32 devices in a mesh: group: 2 (over y), cuts: 4 (over z), probe: 4 (over x, core).
Axes of the slice: x: 2, y: 2, z: 4, core: 2. Of those that a mesh axis runs over, the one named last changes fastest.
Arguments:
- object_slices: float32 [2, 8, 384, 384], P(None, ('group', 'cuts')), parts along dimension 1, may hold values from -1 to 1, as said below
- probe: bfloat16 [4, 128, 128], P('group'), parts along dimension 0, may hold values from -4 to 4
- intensities: float32 [64, 128, 128], P(('group', 'probe')), parts along dimension 0, may hold values from 0.05 to 2
- offsets: int32 [64, 2], P(('group', 'probe')), parts along dimension 0, may hold values from 0 to 256
Outputs:
- object_new: float32 [2, 8, 384, 384], P(None, ('group', 'cuts')), parts along dimension 1
The draws below stay inside these ranges and needn't reach their ends.
There are 2 independent parts, one for each index of `group`. The reference program is written for one: setup_inputs(seed, part) draws one part's arguments, and reference() takes and returns one part's arrays. A program takes and returns all parts, laid end to end along the dimension named above; each array names one. Nothing has to cross between parts.
Inputs may be any that keep to these rules, and one draw needn't show every extreme that they name: `object_slices`: each cell's two components form a complex number of magnitude between exp(-0.8 / 4) and 1.
All inputs are finite; a program needn't handle non-finite values.
Results may differ from the reference program's by a relative error of at most 0.0028.
Values may be sent and summed in bfloat16 or wider, within the bound.
No kernel may reach another device: no remote copies, remote signals or barrier semaphores. Data moves between devices by JAX's collectives and lax.ppermute only.
A program may use at most 64 MiB of HBM per device.

```python
import math
import jax
import jax.numpy as jnp
from jax import lax

WIN = 128
OBJ = 384
SLICES = 4
POSITIONS = 32


def draw_object_slices(key, part):
    key_one, key_two = jax.random.split(jax.random.fold_in(key, 17))
    shape = (SLICES, OBJ, OBJ)
    absorb = jax.random.uniform(key_one, shape, jnp.float32, 0.0, 0.5 / SLICES)
    phase = jax.random.uniform(key_two, shape, jnp.float32, -2.0, 2.0)
    amplitude = jnp.exp(-absorb)
    return jnp.stack([amplitude * jnp.cos(phase), amplitude * jnp.sin(phase)])


def with_ends(entries, key, low, high):
    spot = [jax.random.randint(jax.random.fold_in(key, axis), (), 0, length) for axis, length in enumerate(entries.shape)]
    main_axis = entries.shape.index(max(entries.shape))
    neighbour = spot[:main_axis] + [(spot[main_axis] + 1) % entries.shape[main_axis]] + spot[main_axis + 1:]
    return entries.at[tuple(spot)].set(low).at[tuple(neighbour)].set(high)


def levels(rng, shape, cuts, least, largest):
    loudness = 1.0
    for position, blocks in cuts:
        heights = jax.random.uniform(jax.random.fold_in(jax.random.fold_in(rng, 6), position), (blocks,), jnp.float32, least / len(cuts), largest / len(cuts))
        loudness = loudness * jnp.repeat(jnp.exp(heights), shape[position] // blocks).reshape((-1,) + (1,) * (len(shape) - 1 - position))
    return loudness


def noise(rng, shape, deviation, most, kind=jnp.bfloat16):
    return jnp.clip(deviation * jax.random.normal(rng, shape, jnp.float32), -most, most).astype(kind)


def setup_inputs(seed: int = 0, part: int = 0) -> dict:
    keys = jax.random.split(jax.random.key(seed), 5)
    part_splits = jax.random.split(jax.random.fold_in(keys[4], part), 5)
    return {
        "object_slices": draw_object_slices(jax.random.fold_in(jax.random.fold_in(keys[4], part), 71), part),
        "probe": noise(part_splits[1], (2, WIN, WIN), 0.7, 4.0),
        "intensities": jnp.clip(jnp.exp(math.log(2.0) - 3.6888794 * jax.random.uniform(part_splits[2], (POSITIONS, WIN, WIN), jnp.float32) ** levels(part_splits[2], (POSITIONS, WIN, WIN), ((0, 4),), -0.2, 0.2)), 0.05, 2.0),
        "offsets": with_ends(jax.random.randint(part_splits[3], (POSITIONS, 2), 0, OBJ - WIN + 1), jax.random.fold_in(part_splits[3], 1), 0, OBJ - WIN).astype(jnp.int32),
    }


fresnel_phase = 12.0
step_size = 0.5
regular = 1.0


def fresnel(extent):
    frequency = jnp.fft.fftfreq(extent).astype(jnp.float32)
    angles = -fresnel_phase * frequency * frequency
    line_re = jnp.cos(angles)
    line_im = jnp.sin(angles)
    plane_re = line_re[:, None] * line_re[None, :] - line_im[:, None] * line_im[None, :]
    plane_im = line_re[:, None] * line_im[None, :] + line_im[:, None] * line_re[None, :]
    return plane_re, plane_im


def propagate(value_re, value_im, plane_re, plane_im):
    spectrum = jnp.fft.fft2(lax.complex(value_re, value_im))
    result = jnp.fft.ifft2(spectrum * lax.complex(plane_re, plane_im))
    return jnp.real(result).astype(jnp.float32), jnp.imag(result).astype(jnp.float32)


def reference(object_slices, probe, intensities, offsets):
    obj_re = object_slices[0]
    obj_im = object_slices[1]
    extent = probe.shape[1]
    layers = obj_re.shape[0]
    plane_re, plane_im = fresnel(extent)
    anchor = jnp.zeros((), jnp.int32)

    def one_position(totals, inputs):
        corner, measured = inputs
        start = (anchor, corner[0].astype(jnp.int32), corner[1].astype(jnp.int32))
        window_re = lax.dynamic_slice(obj_re, start, (layers, extent, extent))
        window_im = lax.dynamic_slice(obj_im, start, (layers, extent, extent))

        def forward_step(wave_in, pieces):
            piece_re, piece_im = pieces
            wave_re = wave_in[0].astype(jnp.float32)
            wave_im = wave_in[1].astype(jnp.float32)
            trans_re = piece_re * wave_re - piece_im * wave_im
            trans_im = piece_re * wave_im + piece_im * wave_re
            next_re, next_im = propagate(trans_re, trans_im, plane_re, plane_im)
            return jnp.stack([next_re, next_im]).astype(jnp.bfloat16), wave_in

        final_wave, waves = lax.scan(forward_step, probe, (window_re, window_im))
        last_wave = waves[layers - 1].astype(jnp.float32)
        exit_re = window_re[layers - 1] * last_wave[0] - window_im[layers - 1] * last_wave[1]
        exit_im = window_re[layers - 1] * last_wave[1] + window_im[layers - 1] * last_wave[0]
        far_field = jnp.fft.fft2(lax.complex(exit_re, exit_im), norm="ortho")
        far_re = jnp.real(far_field)
        far_im = jnp.imag(far_field)
        misfit = far_re * far_re + far_im * far_im - measured
        exit_grad = jnp.fft.ifft2(misfit * far_field, norm="ortho")
        start_grad = (jnp.real(exit_grad).astype(jnp.float32), jnp.imag(exit_grad).astype(jnp.float32))

        def backward_step(grads, pieces):
            grad_re, grad_im = grads
            piece_re, piece_im, wave_in = pieces
            wave_f = wave_in.astype(jnp.float32)
            contrib_re = wave_f[0] * grad_re + wave_f[1] * grad_im
            contrib_im = wave_f[0] * grad_im - wave_f[1] * grad_re
            bright = wave_f[0] * wave_f[0] + wave_f[1] * wave_f[1]
            sent_back = jnp.stack([piece_re * grad_re + piece_im * grad_im,
                                   piece_re * grad_im - piece_im * grad_re]).astype(jnp.bfloat16)
            back_f = lax.optimization_barrier(sent_back).astype(jnp.float32)
            new_re, new_im = propagate(back_f[0], back_f[1], plane_re, -plane_im)
            return (new_re, new_im), (contrib_re, contrib_im, bright)

        unused, patches = lax.scan(backward_step, start_grad, (window_re, window_im, waves), reverse=True)
        updated = tuple(
            lax.dynamic_update_slice(running, lax.dynamic_slice(running, start, (layers, extent, extent)) + contrib, start)
            for running, contrib in zip(totals, patches))
        return updated, None

    blank = jnp.zeros_like(obj_re)
    totals, unused = lax.scan(one_position, (blank, blank, blank), (offsets, intensities))
    factor = step_size / (totals[2] + regular)
    return jnp.stack([obj_re - factor * totals[0], obj_im - factor * totals[1]])
```

```python
import functools
import math

import jax
import jax.numpy as jnp
import ml_dtypes
import numpy as np
from jax import lax
from jax.experimental import pallas as pl
from jax.experimental.pallas import tpu as pltpu
from jax.sharding import PartitionSpec as P

fresnel_phase = 12.0
step_size = 0.5
regular = 1.0
wire = jnp.bfloat16
lanes = 128
resident_bytes = 24 * 2**20


def tables(extent):
    k = np.arange(extent)
    dft = np.exp(-2j * np.pi * (np.outer(k, k) % extent) / extent) / math.sqrt(extent)
    f = np.where(k < (extent + 1) // 2, k, k - extent) / extent
    fresnel = dft.conj() @ (np.exp(-1j * fresnel_phase * f * f)[:, None] * dft)

    def split(matrix):
        high = matrix.astype(ml_dtypes.bfloat16)
        low = (matrix - high.astype(np.float64)).astype(ml_dtypes.bfloat16)
        return high, low

    right, left = [], []
    for matrix in (fresnel, dft):
        real = np.block([[matrix.real, matrix.imag], [-matrix.imag, matrix.real]])
        right.append(np.concatenate(split(real), axis=0))
        left.append(np.concatenate(split(real.T), axis=1))
    return np.stack(right), np.stack(left)


def sums_kernel(
    sections, positions, group, pieces, extent, resident,
    place_ref, offsets_own_ref, offsets_other_ref, object_ref, probe_ref, right_ref, left_ref,
    intensity_own, intensity_other, *rest,
):
    piece_refs = rest[:pieces]
    out_ref = rest[pieces]
    staged, field, waves, sums, measured, sems = rest[pieces + 1:]
    own, half = place_ref[0], place_ref[1]
    total = 2 * positions
    side = object_ref.shape[1]
    blocks = side // lanes

    copies = [
        pltpu.make_async_copy(intensity_own, measured.at[pl.ds(half * positions, positions)], sems.at[0]),
        pltpu.make_async_copy(intensity_other, measured.at[pl.ds((1 - half) * positions, positions)], sems.at[1]),
    ]
    for index, piece in enumerate(piece_refs if resident else ()):
        shift, row = place_ref[2 + 2 * index], place_ref[3 + 2 * index]
        height = piece.shape[1]
        copies.append(
            pltpu.make_async_copy(
                piece, staged.at[shift, :, pl.ds(pl.multiple_of(row, 16), height), :], sems.at[2 + index]
            )
        )
    for copy in copies:
        copy.start()

    sums[...] = jnp.zeros_like(sums)

    def corner(position):
        is_own = position // positions == half
        slot = lax.rem(position, positions)
        row = jnp.where(is_own, offsets_own_ref[slot, 0], offsets_other_ref[slot, 0])
        column = jnp.where(is_own, offsets_own_ref[slot, 1], offsets_other_ref[slot, 1])
        first = column // lanes
        second = jnp.minimum(first + 1, blocks - 1)
        return row, first, second, column - first * lanes

    lane_of = lax.broadcasted_iota(jnp.int32, (extent, lanes), 1)

    def start_wave(position, carry):
        shift = corner(position)[3]
        for part in range(2):
            waves[0, position, part] = pltpu.roll(probe_ref[part].astype(jnp.float32), shift, 1)
        return carry

    lax.fori_loop(0, total, start_wave, 0)

    for copy in copies:
        copy.wait()

    def load_slice(index, slot):
        for part in range(2):
            for block in range(blocks):
                field[slot, part, block] = staged[index, part, :, block * lanes:(block + 1) * lanes].astype(jnp.float32)

    def load_own(slot):
        for part in range(2):
            for block in range(blocks):
                field[slot, part, block] = (
                    object_ref[part, :, block * lanes:(block + 1) * lanes].astype(wire).astype(jnp.float32)
                )

    def bring(index):
        def other():
            load_slice(index, index)

        def mine():
            load_own(index)

        lax.cond(index == own, mine, other)

    def bring_all(index, carry):
        bring(index)
        return carry

    if resident:
        lax.fori_loop(0, sections, bring_all, 0)

    def ready(index):
        if resident:
            return index
        copy = pltpu.make_async_copy(piece_refs[0].at[index], staged.at[0], sems.at[2])
        copy.start()
        copy.wait()
        load_slice(0, 0)
        return 0

    def sandwich(values, which):
        rows = jnp.concatenate(
            [jnp.concatenate([re.astype(jnp.bfloat16), im.astype(jnp.bfloat16)], axis=1) for re, im in values], axis=0
        )
        middle = jnp.dot(
            jnp.concatenate([rows, rows], axis=1), right_ref[which], preferred_element_type=jnp.float32
        ).astype(jnp.bfloat16)
        parts = [middle[index * extent:(index + 1) * extent] for index in range(len(values))]
        columns = jnp.concatenate(
            [
                jnp.concatenate([part[:, :extent] for part in parts], axis=1),
                jnp.concatenate([part[:, extent:] for part in parts], axis=1),
            ],
            axis=0,
        )
        result = jnp.dot(
            left_ref[which], jnp.concatenate([columns, columns], axis=0), preferred_element_type=jnp.float32
        )
        return [
            (
                result[:extent, index * extent:(index + 1) * extent],
                result[extent:, index * extent:(index + 1) * extent],
            )
            for index in range(len(values))
        ]

    def through(index, source, first_position):
        values = []
        for member in range(group):
            position = first_position + member
            row, first, second, shift = corner(position)
            mask = lane_of < shift
            window = [
                jnp.where(
                    mask,
                    field[index, part, second, pl.ds(row, extent), :],
                    field[index, part, first, pl.ds(row, extent), :],
                )
                for part in range(2)
            ]
            re = waves[source, position, 0]
            im = waves[source, position, 1]
            values.append((window[0] * re - window[1] * im, window[0] * im + window[1] * re))
        return values

    def keep(values, target, first_position):
        for member, (re, im) in enumerate(values):
            waves[target, first_position + member, 0] = re
            waves[target, first_position + member, 1] = im

    def step(index, source, target):
        slot = ready(index)

        def one_group(number, carry):
            first_position = number * group
            keep(sandwich(through(slot, source, first_position), 0), target, first_position)
            return carry

        lax.fori_loop(0, total // group, one_group, 0)

    def forward(index, carry):
        step(index, (index > own).astype(jnp.int32), (index + 1 > own).astype(jnp.int32))
        return carry

    lax.fori_loop(0, sections - 1, forward, 0)

    last_slot = ready(sections - 1)

    def far_group(number, carry):
        first_position = number * group
        source = (sections - 1 > own).astype(jnp.int32)
        far = sandwich(through(last_slot, source, first_position), 1)
        weighted = []
        for member, (re, im) in enumerate(far):
            misfit = re * re + im * im - measured[first_position + member].astype(jnp.float32)
            weighted.append((misfit * re, -(misfit * im)))
        keep(sandwich(weighted, 1), 1, first_position)
        return carry

    lax.fori_loop(0, total // group, far_group, 0)

    def backward(count, carry):
        step(sections - 1 - count, 1, 1)
        return carry

    lax.fori_loop(0, sections - 1 - own, backward, 0)

    def settle(position, carry):
        row, first, second, shift = corner(position)
        mask = lane_of < shift
        wave_re, wave_im = waves[0, position, 0], waves[0, position, 1]
        grad_re, grad_im = waves[1, position, 0], waves[1, position, 1]
        terms = (
            wave_re * grad_re - wave_im * grad_im,
            -(wave_re * grad_im + wave_im * grad_re),
            wave_re * wave_re + wave_im * wave_im,
        )
        for kind, term in enumerate(terms):
            sums[kind, first, pl.ds(row, extent), :] += jnp.where(mask, 0.0, term)
            sums[kind, second, pl.ds(row, extent), :] += jnp.where(mask, term, 0.0)
        return carry

    lax.fori_loop(0, total, settle, 0)
    for kind in range(3):
        for block in range(blocks):
            out_ref[kind, :, block * lanes:(block + 1) * lanes] = sums[kind, block].astype(wire)


def on_device(object_slices, probe, intensities, offsets):
    own_object = object_slices[:, 0]
    side = own_object.shape[1]
    extent = probe.shape[1]
    positions = offsets.shape[0]
    sections = lax.axis_size("cuts")
    own = lax.axis_index("cuts")
    members = lax.axis_size("probe")
    member = lax.axis_index("probe")
    half_count = members // 2
    half = member // half_count

    across = [(source, (source + half_count) % members) for source in range(members)]
    beside = [(source, source ^ 1) for source in range(members)]

    measured = intensities.astype(wire)
    measured_other = lax.ppermute(measured, "probe", across)
    offsets_other = lax.ppermute(offsets, "probe", across)

    resident = sections * own_object.size * 6 <= resident_bytes
    pieces, places = [], []
    if resident:
        height = side // members
        quarter = lax.dynamic_slice_in_dim(own_object, member * height, height, 1).astype(wire)
        for distance in range(1, sections):
            ring = [(source, (source + distance) % sections) for source in range(sections)]
            first = lax.ppermute(quarter, "cuts", ring)
            opposite = lax.ppermute(first, "probe", across)
            origin = (own - distance) % sections
            for piece, where in (
                (first, member),
                (opposite, (member + half_count) % members),
                (lax.ppermute(first, "probe", beside), member ^ 1),
                (lax.ppermute(opposite, "probe", beside), ((member ^ 1) + half_count) % members),
            ):
                pieces.append(piece)
                places += [origin, where * height]
    else:
        pieces.append(lax.all_gather(own_object.astype(wire), "cuts"))

    right, left = tables(extent)
    scalars = jnp.stack([jnp.asarray(v, jnp.int32) for v in [own, half] + places])
    smem = pl.BlockSpec(memory_space=pltpu.SMEM)
    vmem = pl.BlockSpec(memory_space=pltpu.VMEM)
    anywhere = pl.BlockSpec(memory_space=pl.ANY)
    group = 4
    total = 2 * positions
    blocks = side // lanes
    slots = sections if resident else 1
    own_sums = pl.pallas_call(
        functools.partial(sums_kernel, sections, positions, group, len(pieces), extent, resident),
        out_shape=jax.ShapeDtypeStruct((3, side, side), wire),
        in_specs=[smem, smem, smem] + [vmem] * 4 + [anywhere] * (2 + len(pieces)),
        out_specs=vmem,
        scratch_shapes=[
            pltpu.VMEM((slots, 2, side, side), wire),
            pltpu.VMEM((slots, 2, blocks, side, lanes), jnp.float32),
            pltpu.VMEM((2, total, 2, extent, extent), jnp.float32),
            pltpu.VMEM((3, blocks, side, lanes), jnp.float32),
            pltpu.VMEM((total, extent, extent), wire),
            pltpu.SemaphoreType.DMA((2 + len(pieces),)),
        ],
        compiler_params=pltpu.CompilerParams(vmem_limit_bytes=48 * 2**20),
    )(
        scalars, offsets, offsets_other, own_object, probe, jnp.asarray(right), jnp.asarray(left),
        measured, measured_other, *pieces,
    )
    other_sums = lax.ppermute(own_sums, "probe", beside)
    summed = own_sums.astype(jnp.float32) + other_sums.astype(jnp.float32)
    updated = own_object - (step_size / (summed[2] + regular)) * summed[:2]
    return updated[:, None]


def solution(mesh):
    in_specs = (
        P(None, ("group", "cuts"), None, None),
        P("group", None, None),
        P(("group", "probe"), None, None),
        P(("group", "probe"), None),
    )
    out_specs = P(None, ("group", "cuts"), None, None)
    return jax.shard_map(
        on_device, mesh=mesh, in_specs=in_specs, out_specs=out_specs, check_vma=False
    )
```

```python
import functools
import math

import jax
import jax.numpy as jnp
import ml_dtypes
import numpy as np
from jax import lax
from jax.experimental import pallas as pl
from jax.experimental.pallas import tpu as pltpu
from jax.sharding import PartitionSpec as P

fresnel_phase = 12.0
step_size = 0.5
regular = 1.0
wire = jnp.bfloat16
lanes = 128
first_factor = 1.0554317823341433 * np.exp(1.0168288222118962j)
second_factor = 2.0 / 1.0554317823341433 * np.exp(1.06185831691335j)
dft_factor = 1.1777227895949816 * np.exp(1.1780972450961724j)
resident_bytes = 24 * 2**20


def tables(extent):
    k = np.arange(extent)
    dft = np.exp(-2j * np.pi * (np.outer(k, k) % extent) / extent) / math.sqrt(extent)
    f = np.where(k < (extent + 1) // 2, k, k - extent) / extent
    fresnel = dft.conj() @ (np.exp(-1j * fresnel_phase * f * f)[:, None] * dft)

    def real_form(matrix):
        return np.block([[matrix.real, matrix.imag], [-matrix.imag, matrix.real]]).astype(ml_dtypes.bfloat16)

    last = real_form(dft * dft_factor)
    return np.stack(
        [real_form(fresnel * first_factor), real_form(fresnel * second_factor).T * ml_dtypes.bfloat16(0.5), last, last.T]
    )


def corner_of(half, positions, blocks, offsets_own_ref, offsets_other_ref, position):
    is_own = position // positions == half
    slot = lax.rem(position, positions)
    row = jnp.where(is_own, offsets_own_ref[slot, 0], offsets_other_ref[slot, 0])
    column = jnp.where(is_own, offsets_own_ref[slot, 1], offsets_other_ref[slot, 1])
    first = column // lanes
    return row, first, jnp.minimum(first + 1, blocks - 1), column - first * lanes


def sandwich(values, right, left):
    extent = values[0][0].shape[0]
    rows = jnp.concatenate(
        [jnp.concatenate([re.astype(jnp.bfloat16), im.astype(jnp.bfloat16)], axis=1) for re, im in values], axis=0
    )
    middle = jnp.dot(rows, right, preferred_element_type=jnp.float32).astype(jnp.bfloat16)
    parts = [middle[index * extent:(index + 1) * extent] for index in range(len(values))]
    columns = jnp.concatenate(
        [
            jnp.concatenate([part[:, :extent] for part in parts], axis=1),
            jnp.concatenate([part[:, extent:] for part in parts], axis=1),
        ],
        axis=0,
    )
    result = jnp.dot(left, columns, preferred_element_type=jnp.float32)
    spans = [slice(index * extent, (index + 1) * extent) for index in range(len(values))]
    return [(result[:extent, span], result[extent:, span]) for span in spans]


def through(field, slot, waves, source, corners, chosen):
    extent = waves.shape[-2]
    lane_of = lax.broadcasted_iota(jnp.int32, (extent, lanes), 1)
    values = []
    for position in chosen:
        row, first, second, shift = corners(position)
        mask = lane_of < shift
        window_re, window_im = (
            jnp.where(
                mask, field[slot, part, second, pl.ds(row, extent), :], field[slot, part, first, pl.ds(row, extent), :]
            )
            for part in range(2)
        )
        re, im = waves[source, position, 0], waves[source, position, 1]
        values.append((window_re * re - window_im * im, window_re * im + window_im * re))
    return values


def keep(values, waves, target, chosen):
    for position, (re, im) in zip(chosen, values):
        waves[target, position, 0] = re
        waves[target, position, 1] = im


def in_batches(total, group, batch, work):
    def one_group(number, carry):
        for start in range(0, group, batch):
            work([number * group + start + member for member in range(batch)])
        return carry

    if total == group:
        one_group(0, 0)
    else:
        lax.fori_loop(0, total // group, one_group, 0)


def place_pieces(field, place_ref, first_place, piece_refs):
    for index, piece in enumerate(piece_refs):
        origin = place_ref[first_place + 2 * index]
        row = pl.multiple_of(place_ref[first_place + 2 * index + 1], 16)
        for part in range(2):
            for block in range(field.shape[2]):
                field[origin, part, block, pl.ds(row, piece.shape[1]), :] = (
                    piece[part, :, block * lanes:(block + 1) * lanes].astype(jnp.float32)
                )


def sums_kernel(
    sections, pieces, resident, group, batch,
    place_ref, offsets_own_ref, offsets_other_ref, tables_hbm, object_hbm, probe_ref, measured_own, measured_other, *rest,
):
    piece_refs = rest[:pieces]
    out_ref, field, waves, sums, table_ref, own_ref, sems = rest[pieces:]
    own, half = place_ref[0], place_ref[1]
    total, extent = waves.shape[1], waves.shape[3]
    positions = total // 2
    blocks = sums.shape[1]
    corners = functools.partial(corner_of, half, positions, blocks, offsets_own_ref, offsets_other_ref)

    table_copy = pltpu.make_async_copy(tables_hbm, table_ref, sems.at[0])
    table_copy.start()
    if resident:
        own_copy = pltpu.make_async_copy(object_hbm, own_ref, sems.at[1])
        own_copy.start()

    def start_wave(position, carry):
        shift = corners(position)[3]
        for part in range(2):
            waves[0, position, part] = pltpu.roll(probe_ref[part].astype(jnp.float32), shift, 1)
        return carry

    lax.fori_loop(0, total, start_wave, 0, unroll=4)
    sums[...] = jnp.zeros_like(sums)
    if resident:
        place_pieces(field, place_ref, 2, piece_refs)
        own_copy.wait()
        for part in range(2):
            for block in range(blocks):
                field[own, part, block] = (
                    own_ref[part, :, block * lanes:(block + 1) * lanes].astype(wire).astype(jnp.float32)
                )
    table_copy.wait()

    def ready(index):
        if resident:
            return index
        copy = pltpu.make_async_copy(piece_refs[0].at[index], own_ref, sems.at[1])
        copy.start()
        copy.wait()
        for part in range(2):
            for block in range(blocks):
                field[0, part, block] = own_ref[part, :, block * lanes:(block + 1) * lanes].astype(jnp.float32)
        return 0

    def step(index, source, target):
        slot = ready(index)

        def work(chosen):
            values = through(field, slot, waves, source, corners, chosen)
            keep(sandwich(values, table_ref[0], table_ref[1]), waves, target, chosen)

        in_batches(total, group, batch, work)

    def forward(index, carry):
        step(index, (index > own).astype(jnp.int32), (index + 1 > own).astype(jnp.int32))
        return carry

    lax.fori_loop(0, sections - 1, forward, 0)

    last_slot = ready(sections - 1)
    undo = abs(dft_factor) ** -4

    def far(chosen):
        source = (sections - 1 > own).astype(jnp.int32)
        fields = sandwich(through(field, last_slot, waves, source, corners, chosen), table_ref[2], table_ref[3])
        weighted = []
        for position, (re, im) in zip(chosen, fields):
            is_own = position // positions == half
            slot = lax.rem(position, positions)
            intensity = jnp.where(
                is_own, measured_own[slot].astype(jnp.float32), measured_other[slot].astype(jnp.float32)
            )
            misfit = ((re * re + im * im) * undo - intensity) * undo
            weighted.append((misfit * re, -(misfit * im)))
        keep(sandwich(weighted, table_ref[2], table_ref[3]), waves, 1, chosen)

    in_batches(total, group, batch, far)

    def backward(count, carry):
        step(sections - 1 - count, 1, 1)
        return carry

    lax.fori_loop(0, sections - 1 - own, backward, 0)

    lane_of = lax.broadcasted_iota(jnp.int32, (extent, lanes), 1)

    def settle(position, carry):
        row, first, second, shift = corners(position)
        mask = lane_of < shift
        wave_re, wave_im = waves[0, position, 0], waves[0, position, 1]
        grad_re, grad_im = waves[1, position, 0], waves[1, position, 1]
        terms = (
            wave_re * grad_re - wave_im * grad_im,
            -(wave_re * grad_im + wave_im * grad_re),
            wave_re * wave_re + wave_im * wave_im,
        )
        for kind, term in enumerate(terms):
            sums[kind, first, pl.ds(row, extent), :] += jnp.where(mask, 0.0, term)
            sums[kind, second, pl.ds(row, extent), :] += jnp.where(mask, term, 0.0)
        return carry

    lax.fori_loop(0, total, settle, 0)
    for kind in range(3):
        for block in range(blocks):
            out_ref[kind, :, block * lanes:(block + 1) * lanes] = sums[kind, block].astype(wire)


smem = pl.BlockSpec(memory_space=pltpu.SMEM)
vmem = pl.BlockSpec(memory_space=pltpu.VMEM)
anywhere = pl.BlockSpec(memory_space=pl.ANY)
GROUP, BATCH = 16, 16


def sums_call(sections, positions, extent, side, pieces, resident):
    total = 2 * positions
    group = math.gcd(GROUP, total)
    slice_shape = (2, side // lanes, side, lanes)
    return pl.pallas_call(
        functools.partial(sums_kernel, sections, pieces, resident, group, math.gcd(BATCH, group)),
        out_shape=jax.ShapeDtypeStruct((3, side, side), wire),
        in_specs=[smem] * 3 + [anywhere] * 2 + [vmem] * 3 + [vmem if resident else anywhere] * pieces,
        out_specs=vmem,
        scratch_shapes=[
            pltpu.VMEM((sections if resident else 1,) + slice_shape, jnp.float32),
            pltpu.VMEM((2, total, 2, extent, extent), jnp.float32),
            pltpu.VMEM((3,) + slice_shape[1:], jnp.float32),
            pltpu.VMEM((4, 2 * extent, 2 * extent), jnp.bfloat16),
            pltpu.VMEM((2, side, side), jnp.float32 if resident else wire),
            pltpu.SemaphoreType.DMA((2,)),
        ],
        compiler_params=pltpu.CompilerParams(vmem_limit_bytes=40 * 2**20),
    )


def on_device(object_slices, probe, intensities, offsets):
    own_object = object_slices[:, 0]
    side = own_object.shape[1]
    extent = probe.shape[1]
    positions = offsets.shape[0]
    sections = lax.axis_size("cuts")
    own = lax.axis_index("cuts")
    members = lax.axis_size("probe")
    member = lax.axis_index("probe")
    half_count = members // 2
    half = member // half_count

    across = [(source, (source + half_count) % members) for source in range(members)]
    beside = [(source, source ^ 1) for source in range(members)]

    def scalars(*values):
        return jnp.stack([jnp.asarray(value, jnp.int32) for value in values])

    measured = intensities.astype(wire)
    measured_other = lax.ppermute(measured, "probe", across)
    offsets_other = lax.ppermute(offsets, "probe", across)

    resident = sections & (sections - 1) == 0 and sections * own_object.size * 6 <= resident_bytes
    pieces, places = [], []
    if resident:
        height = side // members
        quarter = lax.dynamic_slice_in_dim(own_object, member * height, height, 1).astype(wire)
        direct = {}
        for distance in ([2,3,1]):
            swap = [(source, source ^ distance) for source in range(sections)]
            direct[distance] = lax.ppermute(quarter, "cuts", swap)
        for distance in sorted(direct):
            opposite = lax.ppermute(direct[distance], "probe", across)
            for piece, where in (
                (direct[distance], member),
                (opposite, (member + half_count) % members),
                (lax.ppermute(direct[distance], "probe", beside), member ^ 1),
                (lax.ppermute(opposite, "probe", beside), ((member ^ 1) + half_count) % members),
            ):
                pieces.append(piece)
                places += [own ^ distance, where * height]
    else:
        pieces.append(lax.all_gather(own_object.astype(wire), "cuts"))
    own_sums = sums_call(sections, positions, extent, side, len(pieces), resident)(
        scalars(own, half, *places), offsets, offsets_other, jnp.asarray(tables(extent)), own_object, probe,
        measured, measured_other, *pieces,
    )
    other_sums = lax.ppermute(own_sums, "probe", beside)
    summed = own_sums.astype(jnp.float32) + other_sums.astype(jnp.float32)
    updated = own_object - (step_size / (summed[2] + regular)) * summed[:2]
    return updated[:, None]


def solution(mesh):
    in_specs = (
        P(None, ("group", "cuts"), None, None),
        P("group", None, None),
        P(("group", "probe"), None, None),
        P(("group", "probe"), None),
    )
    out_specs = P(None, ("group", "cuts"), None, None)
    return jax.shard_map(
        on_device, mesh=mesh, in_specs=in_specs, out_specs=out_specs, check_vma=False
    )
```

```python
import functools
import math

import jax
import jax.numpy as jnp
import ml_dtypes
import numpy as np
from jax import lax
from jax.experimental import pallas as pl
from jax.experimental.pallas import tpu as pltpu
from jax.sharding import PartitionSpec as P

fresnel_phase = 12.0
step_size = 0.5
regular = 1.0
wire = jnp.bfloat16
lanes = 128
first_factor = 1.0554317823341433 * np.exp(1.0168288222118962j)
second_factor = 2.0 / 1.0554317823341433 * np.exp(1.06185831691335j)
dft_factor = 1.1777227895949816 * np.exp(1.1780972450961724j)
resident_bytes = 24 * 2**20


def tables(extent):
    k = np.arange(extent)
    dft = np.exp(-2j * np.pi * (np.outer(k, k) % extent) / extent) / math.sqrt(extent)
    f = np.where(k < (extent + 1) // 2, k, k - extent) / extent
    fresnel = dft.conj() @ (np.exp(-1j * fresnel_phase * f * f)[:, None] * dft)

    def real_form(matrix):
        return np.block([[matrix.real, matrix.imag], [-matrix.imag, matrix.real]]).astype(ml_dtypes.bfloat16)

    last = real_form(dft * dft_factor)
    return np.stack(
        [real_form(fresnel * first_factor), real_form(fresnel * second_factor).T * ml_dtypes.bfloat16(0.5), last, last.T]
    )


def corner_of(half, positions, blocks, offsets_ref, position):
    source = (position // positions != half).astype(jnp.int32)
    slot = lax.rem(position, positions)
    row, column = offsets_ref[source, slot, 0], offsets_ref[source, slot, 1]
    first = column // lanes
    return row, first, jnp.minimum(first + 1, blocks - 1), column - first * lanes


def sandwich(values, right, left):
    extent = values[0][0].shape[0]
    rows = jnp.concatenate(
        [jnp.concatenate([re.astype(jnp.bfloat16), im.astype(jnp.bfloat16)], axis=1) for re, im in values], axis=0
    )
    middle = jnp.dot(rows, right, preferred_element_type=jnp.float32).astype(jnp.bfloat16)
    parts = [middle[index * extent:(index + 1) * extent] for index in range(len(values))]
    columns = jnp.concatenate(
        [
            jnp.concatenate([part[:, :extent] for part in parts], axis=1),
            jnp.concatenate([part[:, extent:] for part in parts], axis=1),
        ],
        axis=0,
    )
    result = jnp.dot(left, columns, preferred_element_type=jnp.float32)
    spans = [slice(index * extent, (index + 1) * extent) for index in range(len(values))]
    return [(result[:extent, span], result[extent:, span]) for span in spans]


def through(field, slot, waves, source, corners, chosen):
    extent = waves.shape[-2]
    lane_of = lax.broadcasted_iota(jnp.int32, (extent, lanes), 1)
    values = []
    for position in chosen:
        row, first, second, shift = corners(position)
        mask = lane_of < shift
        window_re, window_im = (
            jnp.where(
                mask, field[slot, part, second, pl.ds(row, extent), :], field[slot, part, first, pl.ds(row, extent), :]
            )
            for part in range(2)
        )
        re, im = waves[source, position, 0], waves[source, position, 1]
        values.append((window_re * re - window_im * im, window_re * im + window_im * re))
    return values


def keep(values, waves, target, chosen):
    for position, (re, im) in zip(chosen, values):
        waves[target, position, 0] = re
        waves[target, position, 1] = im


def in_batches(total, group, batch, work):
    def one_group(number, carry):
        for start in range(0, group, batch):
            work([number * group + start + member for member in range(batch)])
        return carry

    if total == group:
        one_group(0, 0)
    else:
        lax.fori_loop(0, total // group, one_group, 0)


def place_pieces(field, place_ref, first_place, piece_refs):
    for index, piece in enumerate(piece_refs):
        origin = place_ref[first_place + 2 * index]
        row = pl.multiple_of(place_ref[first_place + 2 * index + 1], 16)
        for part in range(2):
            for block in range(field.shape[2]):
                field[origin, part, block, pl.ds(row, piece.shape[1]), :] = (
                    piece[part, :, block * lanes:(block + 1) * lanes].astype(jnp.float32)
                )


def sums_kernel(
    sections, pieces, resident, group, batch,
    place_ref, tables_hbm, object_hbm, probe_hbm, measured_own, measured_other, *rest,
):
    piece_refs = rest[:pieces]
    out_ref, field, waves, sums, table_ref, own_ref, probe_ref, numbers, offsets_ref, sems = rest[pieces:]
    own, half = place_ref[0], place_ref[1]
    total, extent = waves.shape[1], waves.shape[3]
    positions = total // 2
    blocks = sums.shape[1]
    corners = functools.partial(corner_of, half, positions, blocks, offsets_ref)

    for source, measured in enumerate((measured_own, measured_other)):
        numbers[source] = measured[positions, :numbers.shape[1]].astype(jnp.float32).astype(jnp.int32)
    offsets_copy = pltpu.make_async_copy(numbers, offsets_ref, sems.at[3])
    offsets_copy.start()

    probe_copy = pltpu.make_async_copy(probe_hbm, probe_ref, sems.at[2])
    probe_copy.start()
    table_copy = pltpu.make_async_copy(tables_hbm, table_ref, sems.at[0])
    table_copy.start()
    if resident:
        own_copy = pltpu.make_async_copy(object_hbm, own_ref, sems.at[1])
        own_copy.start()
        place_pieces(field, place_ref, 2, piece_refs)
    sums[...] = jnp.zeros_like(sums)
    probe_copy.wait()
    offsets_copy.wait()

    def start_wave(position, carry):
        shift = corners(position)[3]
        for part in range(2):
            waves[0, position, part] = pltpu.roll(probe_ref[part].astype(jnp.float32), shift, 1)
        return carry

    lax.fori_loop(0, total, start_wave, 0, unroll=4)
    if resident:
        own_copy.wait()
        for part in range(2):
            for block in range(blocks):
                field[own, part, block] = (
                    own_ref[part, :, block * lanes:(block + 1) * lanes].astype(wire).astype(jnp.float32)
                )
    table_copy.wait()

    def ready(index):
        if resident:
            return index
        copy = pltpu.make_async_copy(piece_refs[0].at[index], own_ref, sems.at[1])
        copy.start()
        copy.wait()
        for part in range(2):
            for block in range(blocks):
                field[0, part, block] = own_ref[part, :, block * lanes:(block + 1) * lanes].astype(jnp.float32)
        return 0

    def step(index, source, target):
        slot = ready(index)

        def work(chosen):
            values = through(field, slot, waves, source, corners, chosen)
            keep(sandwich(values, table_ref[0], table_ref[1]), waves, target, chosen)

        in_batches(total, group, batch, work)

    def forward(index, carry):
        step(index, (index > own).astype(jnp.int32), (index + 1 > own).astype(jnp.int32))
        return carry

    lax.fori_loop(0, sections - 1, forward, 0)

    last_slot = ready(sections - 1)
    undo = abs(dft_factor) ** -4

    def far(chosen):
        source = (sections - 1 > own).astype(jnp.int32)
        fields = sandwich(through(field, last_slot, waves, source, corners, chosen), table_ref[2], table_ref[3])
        weighted = []
        for position, (re, im) in zip(chosen, fields):
            is_own = position // positions == half
            slot = lax.rem(position, positions)
            intensity = jnp.where(
                is_own, measured_own[slot].astype(jnp.float32), measured_other[slot].astype(jnp.float32)
            )
            misfit = ((re * re + im * im) * undo - intensity) * undo
            weighted.append((misfit * re, -(misfit * im)))
        keep(sandwich(weighted, table_ref[2], table_ref[3]), waves, 1, chosen)

    in_batches(total, group, batch, far)

    def backward(count, carry):
        step(sections - 1 - count, 1, 1)
        return carry

    lax.fori_loop(0, sections - 1 - own, backward, 0)

    lane_of = lax.broadcasted_iota(jnp.int32, (extent, lanes), 1)

    def settle(position, carry):
        row, first, second, shift = corners(position)
        mask = lane_of < shift
        wave_re, wave_im = waves[0, position, 0], waves[0, position, 1]
        grad_re, grad_im = waves[1, position, 0], waves[1, position, 1]
        terms = (
            wave_re * grad_re - wave_im * grad_im,
            -(wave_re * grad_im + wave_im * grad_re),
            wave_re * wave_re + wave_im * wave_im,
        )
        for kind, term in enumerate(terms):
            sums[kind, first, pl.ds(row, extent), :] += jnp.where(mask, 0.0, term)
            sums[kind, second, pl.ds(row, extent), :] += jnp.where(mask, term, 0.0)
        return carry

    lax.fori_loop(0, total, settle, 0)
    for kind in range(3):
        for block in range(blocks):
            out_ref[kind, :, block * lanes:(block + 1) * lanes] = sums[kind, block].astype(wire)


smem = pl.BlockSpec(memory_space=pltpu.SMEM)
vmem = pl.BlockSpec(memory_space=pltpu.VMEM)
anywhere = pl.BlockSpec(memory_space=pl.ANY)
hbm = pl.BlockSpec(memory_space=pltpu.HBM)
GROUP, BATCH = 16, 16


def sums_call(sections, positions, extent, side, pieces, resident):
    total = 2 * positions
    group = math.gcd(GROUP, total)
    slice_shape = (2, side // lanes, side, lanes)
    return pl.pallas_call(
        functools.partial(sums_kernel, sections, pieces, resident, group, math.gcd(BATCH, group)),
        out_shape=jax.ShapeDtypeStruct((3, side, side), wire),
        in_specs=[smem] + [hbm] * 3 + [vmem] * 2 + [vmem if resident else anywhere] * pieces,
        out_specs=vmem,
        scratch_shapes=[
            pltpu.VMEM((sections if resident else 1,) + slice_shape, jnp.float32),
            pltpu.VMEM((2, total, 2, extent, extent), jnp.float32),
            pltpu.VMEM((3,) + slice_shape[1:], jnp.float32),
            pltpu.VMEM((4, 2 * extent, 2 * extent), jnp.bfloat16),
            pltpu.VMEM((2, side, side), jnp.float32 if resident else wire),
            pltpu.VMEM((2, extent, extent), jnp.bfloat16),
            pltpu.VMEM((2, -(-positions // 16) * 16, extent), jnp.int32),
            pltpu.SMEM((2, -(-positions // 16) * 16, extent), jnp.int32),
            pltpu.SemaphoreType.DMA((4,)),
        ],
        compiler_params=pltpu.CompilerParams(vmem_limit_bytes=40 * 2**20),
    )


def on_device(object_slices, probe, intensities, offsets):
    own_object = object_slices[:, 0]
    side = own_object.shape[1]
    extent = probe.shape[1]
    positions = offsets.shape[0]
    sections = lax.axis_size("cuts")
    own = lax.axis_index("cuts")
    members = lax.axis_size("probe")
    member = lax.axis_index("probe")
    half_count = members // 2
    half = member // half_count

    across = [(source, (source + half_count) % members) for source in range(members)]
    beside = [(source, source ^ 1) for source in range(members)]

    def scalars(*values):
        return jnp.stack([jnp.asarray(value, jnp.int32) for value in values])

    plane = jnp.pad(offsets.astype(wire), ((0, extent - positions), (0, extent - offsets.shape[1])))
    measured = jnp.concatenate([intensities.astype(wire), plane[None]])
    measured_other = lax.ppermute(measured, "probe", across)

    resident = sections & (sections - 1) == 0 and sections * own_object.size * 6 <= resident_bytes
    pieces, places = [], []
    if resident:
        height = side // members
        quarter = lax.dynamic_slice_in_dim(own_object, member * height, height, 1).astype(wire)
        swap = lambda distance: [(source, source ^ distance) for source in range(sections)]
        go = lambda value, distance: lax.ppermute(value, "cuts", swap(distance))
        over = lambda value: lax.ppermute(value, "probe", across)
        direct = {2: go(quarter, 2), 1: go(quarter, 1)}
        direct[1], measured_other = lax.optimization_barrier((direct[1], measured_other))
        direct[3] = go(direct[2], 1)
        opposite = {distance: over(direct[distance]) for distance in (2, 1)}
        opposite[3] = go(opposite[2], 1)
        for distance in (2, 1, 3):
            for piece, where in (
                (direct[distance], member),
                (opposite[distance], (member + half_count) % members),
                (lax.ppermute(direct[distance], "probe", beside), member ^ 1),
                (lax.ppermute(opposite[distance], "probe", beside), ((member ^ 1) + half_count) % members),
            ):
                pieces.append(piece)
                places += [own ^ distance, where * height]
    else:
        pieces.append(lax.all_gather(own_object.astype(wire), "cuts"))
    own_sums = sums_call(sections, positions, extent, side, len(pieces), resident)(
        scalars(own, half, *places), jnp.asarray(tables(extent)), own_object, probe,
        measured, measured_other, *pieces,
    )
    other_sums = lax.ppermute(own_sums, "probe", beside)
    summed = own_sums.astype(jnp.float32) + other_sums.astype(jnp.float32)
    updated = own_object - (step_size / (summed[2] + regular)) * summed[:2]
    return updated[:, None]


def solution(mesh):
    in_specs = (
        P(None, ("group", "cuts"), None, None),
        P("group", None, None),
        P(("group", "probe"), None, None),
        P(("group", "probe"), None),
    )
    out_specs = P(None, ("group", "cuts"), None, None)
    return jax.shard_map(
        on_device, mesh=mesh, in_specs=in_specs, out_specs=out_specs, check_vma=False
    )
```

```python
import functools
import math

import jax
import jax.numpy as jnp
import ml_dtypes
import numpy as np
from jax import lax
from jax.experimental import pallas as pl
from jax.experimental.pallas import tpu as pltpu
from jax.sharding import PartitionSpec as P

fresnel_phase = 12.0
step_size = 0.5
regular = 1.0
wire = jnp.bfloat16
lanes = 128
first_factor = 1.0554317823341433 * np.exp(1.0168288222118962j)
second_factor = 2.0 / 1.0554317823341433 * np.exp(1.06185831691335j)
dft_factor = 1.1777227895949816 * np.exp(1.1780972450961724j)
resident_bytes = 24 * 2**20


def tables(extent):
    k = np.arange(extent)
    dft = np.exp(-2j * np.pi * (np.outer(k, k) % extent) / extent) / math.sqrt(extent)
    f = np.where(k < (extent + 1) // 2, k, k - extent) / extent
    fresnel = dft.conj() @ (np.exp(-1j * fresnel_phase * f * f)[:, None] * dft)

    def real_form(matrix):
        return np.block([[matrix.real, matrix.imag], [-matrix.imag, matrix.real]]).astype(ml_dtypes.bfloat16)

    last = real_form(dft * dft_factor)
    return np.stack(
        [real_form(fresnel * first_factor), real_form(fresnel * second_factor).T * ml_dtypes.bfloat16(0.5), last, last.T]
    )


def corner_of(half, positions, blocks, offsets_ref, position):
    source = (position // positions != half).astype(jnp.int32)
    slot = lax.rem(position, positions)
    row, column = offsets_ref[source, slot, 0], offsets_ref[source, slot, 1]
    first = column // lanes
    return row, first, jnp.minimum(first + 1, blocks - 1), column - first * lanes


def sandwich(values, right, left):
    extent = values[0][0].shape[0]
    rows = jnp.concatenate(
        [jnp.concatenate([re.astype(jnp.bfloat16), im.astype(jnp.bfloat16)], axis=1) for re, im in values], axis=0
    )
    strips = math.gcd(len(values), 4)
    height = rows.shape[0] // strips
    middle = jnp.concatenate(
        [
            jnp.dot(rows[strip * height:(strip + 1) * height], right, preferred_element_type=jnp.float32).astype(
                jnp.bfloat16
            )
            for strip in range(strips)
        ],
        axis=0,
    )
    parts = [middle[index * extent:(index + 1) * extent] for index in range(len(values))]
    columns = jnp.concatenate(
        [
            jnp.concatenate([part[:, :extent] for part in parts], axis=1),
            jnp.concatenate([part[:, extent:] for part in parts], axis=1),
        ],
        axis=0,
    )
    result = jnp.dot(left, columns, preferred_element_type=jnp.float32)
    spans = [slice(index * extent, (index + 1) * extent) for index in range(len(values))]
    return [(result[:extent, span], result[extent:, span]) for span in spans]


def through(field, slot, waves, source, corners, chosen):
    extent = waves.shape[-2]
    lane_of = lax.broadcasted_iota(jnp.int32, (extent, lanes), 1)
    values = []
    for position in chosen:
        row, first, second, shift = corners(position)
        mask = lane_of < shift
        window_re, window_im = (
            jnp.where(
                mask, field[slot, part, second, pl.ds(row, extent), :], field[slot, part, first, pl.ds(row, extent), :]
            )
            for part in range(2)
        )
        re, im = waves[source, position, 0], waves[source, position, 1]
        values.append((window_re * re - window_im * im, window_re * im + window_im * re))
    return values


def keep(values, waves, target, chosen):
    for position, (re, im) in zip(chosen, values):
        waves[target, position, 0] = re
        waves[target, position, 1] = im


def in_batches(total, group, batch, work):
    def one_group(number, carry):
        for start in range(0, group, batch):
            work([number * group + start + member for member in range(batch)])
        return carry

    if total == group:
        one_group(0, 0)
    else:
        lax.fori_loop(0, total // group, one_group, 0)


def place_pieces(field, place_ref, first_place, piece_refs):
    for index, piece in enumerate(piece_refs):
        origin = place_ref[first_place + 2 * index]
        row = pl.multiple_of(place_ref[first_place + 2 * index + 1], 16)
        for part in range(2):
            for block in range(field.shape[2]):
                field[origin, part, block, pl.ds(row, piece.shape[1]), :] = (
                    piece[part, :, block * lanes:(block + 1) * lanes].astype(jnp.float32)
                )


def sums_kernel(
    sections, pieces, resident, group, batch,
    place_ref, tables_hbm, object_hbm, probe_hbm, measured_own, measured_other, *rest,
):
    piece_refs = rest[:pieces]
    out_ref, field, waves, sums, table_ref, own_ref, probe_ref, numbers, offsets_ref, sems = rest[pieces:]
    own, half = place_ref[0], place_ref[1]
    total, extent = waves.shape[1], waves.shape[3]
    positions = total // 2
    blocks = sums.shape[1]
    corners = functools.partial(corner_of, half, positions, blocks, offsets_ref)

    for source, measured in enumerate((measured_own, measured_other)):
        numbers[source] = measured[positions, :numbers.shape[1]].astype(jnp.float32).astype(jnp.int32)
    offsets_copy = pltpu.make_async_copy(numbers, offsets_ref, sems.at[3])
    offsets_copy.start()

    probe_copy = pltpu.make_async_copy(probe_hbm, probe_ref, sems.at[2])
    probe_copy.start()
    table_copy = pltpu.make_async_copy(tables_hbm, table_ref, sems.at[0])
    table_copy.start()
    if resident:
        own_copy = pltpu.make_async_copy(object_hbm, own_ref, sems.at[1])
        own_copy.start()
        place_pieces(field, place_ref, 2, piece_refs)
    sums[...] = jnp.zeros_like(sums)
    probe_copy.wait()
    offsets_copy.wait()

    def start_wave(position, carry):
        shift = corners(position)[3]
        for part in range(2):
            waves[0, position, part] = pltpu.roll(probe_ref[part].astype(jnp.float32), shift, 1)
        return carry

    lax.fori_loop(0, total, start_wave, 0, unroll=16)
    if resident:
        own_copy.wait()
        for part in range(2):
            for block in range(blocks):
                field[own, part, block] = (
                    own_ref[part, :, block * lanes:(block + 1) * lanes].astype(wire).astype(jnp.float32)
                )
    table_copy.wait()

    def ready(index):
        if resident:
            return index
        copy = pltpu.make_async_copy(piece_refs[0].at[index], own_ref, sems.at[1])
        copy.start()
        copy.wait()
        for part in range(2):
            for block in range(blocks):
                field[0, part, block] = own_ref[part, :, block * lanes:(block + 1) * lanes].astype(jnp.float32)
        return 0

    def step(index, source, target):
        slot = ready(index)

        def work(chosen):
            values = through(field, slot, waves, source, corners, chosen)
            keep(sandwich(values, table_ref[0], table_ref[1]), waves, target, chosen)

        in_batches(total, group, batch, work)

    def forward(index, carry):
        step(index, (index > own).astype(jnp.int32), (index + 1 > own).astype(jnp.int32))
        return carry

    lax.fori_loop(0, sections - 1, forward, 0)

    last_slot = ready(sections - 1)
    undo = abs(dft_factor) ** -4

    def far(chosen):
        source = (sections - 1 > own).astype(jnp.int32)
        fields = sandwich(through(field, last_slot, waves, source, corners, chosen), table_ref[2], table_ref[3])
        weighted = []
        for position, (re, im) in zip(chosen, fields):
            is_own = position // positions == half
            slot = lax.rem(position, positions)
            intensity = jnp.where(
                is_own, measured_own[slot].astype(jnp.float32), measured_other[slot].astype(jnp.float32)
            )
            misfit = ((re * re + im * im) * undo - intensity) * undo
            weighted.append((misfit * re, -(misfit * im)))
        keep(sandwich(weighted, table_ref[2], table_ref[3]), waves, 1, chosen)

    in_batches(total, group, batch, far)

    def backward(count, carry):
        step(sections - 1 - count, 1, 1)
        return carry

    lax.fori_loop(0, sections - 1 - own, backward, 0)

    lane_of = lax.broadcasted_iota(jnp.int32, (extent, lanes), 1)

    def settle(position, carry):
        row, first, second, shift = corners(position)
        mask = lane_of < shift
        wave_re, wave_im = waves[0, position, 0], waves[0, position, 1]
        grad_re, grad_im = waves[1, position, 0], waves[1, position, 1]
        terms = (
            wave_re * grad_re - wave_im * grad_im,
            -(wave_re * grad_im + wave_im * grad_re),
            wave_re * wave_re + wave_im * wave_im,
        )
        for kind, term in enumerate(terms):
            sums[kind, first, pl.ds(row, extent), :] += jnp.where(mask, 0.0, term)
            sums[kind, second, pl.ds(row, extent), :] += jnp.where(mask, term, 0.0)
        return carry

    lax.fori_loop(0, total, settle, 0, unroll=4)
    for kind in range(3):
        for block in range(blocks):
            out_ref[kind, :, block * lanes:(block + 1) * lanes] = sums[kind, block].astype(wire)


smem = pl.BlockSpec(memory_space=pltpu.SMEM)
vmem = pl.BlockSpec(memory_space=pltpu.VMEM)
anywhere = pl.BlockSpec(memory_space=pl.ANY)
hbm = pl.BlockSpec(memory_space=pltpu.HBM)
GROUP, BATCH = 16, 16


def sums_call(sections, positions, extent, side, pieces, resident):
    total = 2 * positions
    group = math.gcd(GROUP, total)
    slice_shape = (2, side // lanes, side, lanes)
    return pl.pallas_call(
        functools.partial(sums_kernel, sections, pieces, resident, group, math.gcd(BATCH, group)),
        out_shape=jax.ShapeDtypeStruct((3, side, side), wire),
        in_specs=[smem] + [hbm] * 3 + [vmem] * 2 + [vmem if resident else anywhere] * pieces,
        out_specs=vmem,
        scratch_shapes=[
            pltpu.VMEM((sections if resident else 1,) + slice_shape, jnp.float32),
            pltpu.VMEM((2, total, 2, extent, extent), jnp.float32),
            pltpu.VMEM((3,) + slice_shape[1:], jnp.float32),
            pltpu.VMEM((4, 2 * extent, 2 * extent), jnp.bfloat16),
            pltpu.VMEM((2, side, side), jnp.float32 if resident else wire),
            pltpu.VMEM((2, extent, extent), jnp.bfloat16),
            pltpu.VMEM((2, -(-positions // 16) * 16, extent), jnp.int32),
            pltpu.SMEM((2, -(-positions // 16) * 16, extent), jnp.int32),
            pltpu.SemaphoreType.DMA((4,)),
        ],
        compiler_params=pltpu.CompilerParams(vmem_limit_bytes=40 * 2**20),
    )


def on_device(object_slices, probe, intensities, offsets):
    own_object = object_slices[:, 0]
    side = own_object.shape[1]
    extent = probe.shape[1]
    positions = offsets.shape[0]
    sections = lax.axis_size("cuts")
    own = lax.axis_index("cuts")
    members = lax.axis_size("probe")
    member = lax.axis_index("probe")
    half_count = members // 2
    half = member // half_count

    across = [(source, (source + half_count) % members) for source in range(members)]
    beside = [(source, source ^ 1) for source in range(members)]

    def scalars(*values):
        return jnp.stack([jnp.asarray(value, jnp.int32) for value in values])

    plane = jnp.pad(offsets.astype(wire), ((0, extent - positions), (0, extent - offsets.shape[1])))
    measured = jnp.concatenate([intensities.astype(wire), plane[None]])
    measured_other = lax.ppermute(measured, "probe", across)

    resident = sections & (sections - 1) == 0 and sections * own_object.size * 6 <= resident_bytes
    pieces, places = [], []
    if resident:
        height = side // members
        quarter = lax.dynamic_slice_in_dim(own_object, member * height, height, 1).astype(wire)
        swap = lambda distance: [(source, source ^ distance) for source in range(sections)]
        go = lambda value, distance: lax.ppermute(value, "cuts", swap(distance))
        over = lambda value: lax.ppermute(value, "probe", across)
        direct = {2: go(quarter, 2), 1: go(quarter, 1)}
        direct[1], measured_other = lax.optimization_barrier((direct[1], measured_other))
        direct[3] = go(direct[2], 1)
        opposite = {distance: over(direct[distance]) for distance in (2, 1)}
        opposite[3] = go(opposite[2], 1)
        for distance in (2, 1, 3):
            for piece, where in (
                (direct[distance], member),
                (opposite[distance], (member + half_count) % members),
                (lax.ppermute(direct[distance], "probe", beside), member ^ 1),
                (lax.ppermute(opposite[distance], "probe", beside), ((member ^ 1) + half_count) % members),
            ):
                pieces.append(piece)
                places += [own ^ distance, where * height]
    else:
        pieces.append(lax.all_gather(own_object.astype(wire), "cuts"))
    own_sums = sums_call(sections, positions, extent, side, len(pieces), resident)(
        scalars(own, half, *places), jnp.asarray(tables(extent)), own_object, probe,
        measured, measured_other, *pieces,
    )
    other_sums = lax.ppermute(own_sums, "probe", beside)
    summed = own_sums.astype(jnp.float32) + other_sums.astype(jnp.float32)
    updated = own_object - (step_size / (summed[2] + regular)) * summed[:2]
    return updated[:, None]


def solution(mesh):
    in_specs = (
        P(None, ("group", "cuts"), None, None),
        P("group", None, None),
        P(("group", "probe"), None, None),
        P(("group", "probe"), None),
    )
    out_specs = P(None, ("group", "cuts"), None, None)
    return jax.shard_map(
        on_device, mesh=mesh, in_specs=in_specs, out_specs=out_specs, check_vma=False
    )
```
